768 devices in a mesh: row: 12 (over z_lo, core), col: 64 (over x, y, z_hi).
Axes of the slice: x: 4, y: 8, z: 12 (z_hi: 2, z_lo: 6; z = z_hi * 6 + z_lo), core: 2. Of those that a mesh axis runs over, the one named last changes fastest.
Arguments:
- x_window: float32 [1536, 122880], P('row', 'col'), may hold values from -6 to 6
- square_rows: float32 [3072, 122880], P('row', 'col'), may hold values from -0.3125 to 0.3125
- block_rank: int32 [12, 960], P('row', 'col'), may hold values from 0 to 14, as said below
- block_count: int32 [12, 64], P('row', 'col'), may hold values from 3 to 15, as said below
- panel_order: int32 [3], replicated, may hold values from 0 to 23, as said below
Outputs:
- updated: float32 [1536, 122880], P('row', 'col')
- total_square: float32 [], replicated
The draws below stay inside these ranges and needn't reach their ends.
Inputs may be any that keep to these rules, and one draw needn't show every extreme that they name: `block_rank`: in each tile the 15 ranks are a permutation of 0 to 14; blocks in block columns of the form k(w) take the lowest ranks of their tile. `block_count`: skewed over tiles; some tile is full. `panel_order`: distinct values; the largest window row is always among them.
All inputs are finite; a program needn't handle non-finite values.
Results may differ from the reference program's by a relative error of at most 0.00045.
Values sent between devices are 32-bit elements; how exact they have to be, the bound alone decides.
A program may use at most 32 MiB of HBM per device.

```python
import jax
import jax.numpy as jnp
from jax import lax

BLOCK_WIDTH = 128
TILE_COLS = 15
SLAB_ROWS = 1
WIN_ROWS = 2
ROUNDS = 3
MATRIX_ORDER = 122880
N_ROW = 12
N_COL = 64


def draw_block_rank(key, part):
    key = jax.random.fold_in(key, 11)
    cells = SLAB_ROWS * TILE_COLS
    all_blocks = TILE_COLS * N_COL
    window_count = WIN_ROWS * N_ROW
    panel_cols = jnp.arange(window_count, dtype=jnp.int32) * all_blocks // window_count
    is_panel = jnp.any(jnp.arange(all_blocks, dtype=jnp.int32)[:, None] == panel_cols[None, :], axis=1)
    offset = jnp.where(is_panel, 0, 1 << 16).astype(jnp.int32).reshape(N_COL, TILE_COLS)
    scores = jax.random.randint(key, (N_ROW, SLAB_ROWS, N_COL, TILE_COLS), 0, 1 << 16)
    scores = scores + offset[None, None, :, :]
    scores = scores.transpose(0, 2, 1, 3).reshape(N_ROW, N_COL, cells)
    scores = scores * cells + jnp.arange(cells, dtype=jnp.int32)
    ranks = jnp.argsort(jnp.argsort(scores, axis=-1), axis=-1).astype(jnp.int32)
    ranks = ranks.reshape(N_ROW, N_COL, SLAB_ROWS, TILE_COLS).transpose(0, 2, 1, 3)
    return ranks.reshape(N_ROW * SLAB_ROWS, N_COL * TILE_COLS)


def draw_block_count(key, part):
    key = jax.random.fold_in(key, 23)
    cells = SLAB_ROWS * TILE_COLS
    lowest = max(1, cells // 4)
    first, second = jax.random.split(key)
    level = jax.random.randint(first, (N_ROW * N_COL,), 0, 1024)
    counts = lowest + (cells - lowest) * level * level // (1023 * 1023)
    chosen = jax.random.randint(second, (), 0, N_ROW * N_COL)
    counts = jnp.where(jnp.arange(N_ROW * N_COL) == chosen, cells, counts)
    return counts.astype(jnp.int32).reshape(N_ROW, N_COL)


def draw_panel_order(key, part):
    key = jax.random.fold_in(key, 37)
    first, second = jax.random.split(key)
    window_count = WIN_ROWS * N_ROW
    shuffled = jax.random.permutation(first, jnp.arange(window_count - 1, dtype=jnp.int32))
    picked = jnp.concatenate([shuffled[:ROUNDS - 1], jnp.full((1,), window_count - 1, jnp.int32)])
    return jax.random.permutation(second, picked).astype(jnp.int32)


def block_levels(rng, dims, cuts, low, top_value):
    loudness, own = 1.0, jax.random.fold_in(rng, 6)
    for dim, shards_of in cuts:
        steps = jnp.exp(jax.random.uniform(jax.random.fold_in(own, dim), (shards_of,), jnp.float32, low / len(cuts), top_value / len(cuts)))
        loudness = loudness * jnp.repeat(steps, dims[dim] // shards_of).reshape([-1 if axis == dim else 1 for axis in range(len(dims))])
    return loudness


def scatter_about(stream_key, dims, width, reach, pieces=(), kind=jnp.bfloat16):
    drawn = width * jax.random.normal(stream_key, dims, jnp.float32)
    if pieces:
        drawn = drawn * block_levels(stream_key, dims, pieces, -0.22, 0.18)
    return jnp.clip(drawn, -reach, reach).astype(kind)


def setup_inputs(seed: int = 0) -> dict:
    seeds = jax.random.split(jax.random.key(seed), 6)
    return {
        "x_window": scatter_about(seeds[0], (N_ROW * SLAB_ROWS * BLOCK_WIDTH, MATRIX_ORDER), 1.0, 6.0, ((0, 12), (1, 64)), jnp.float32),
        "square_rows": scatter_about(seeds[1], (N_ROW * WIN_ROWS * BLOCK_WIDTH, MATRIX_ORDER), (ROUNDS * BLOCK_WIDTH) ** -0.5, 0.3125, ((0, 12), (1, 64)), jnp.float32),
        "block_rank": draw_block_rank(jax.random.fold_in(seeds[5], 71), 0),
        "block_count": draw_block_count(jax.random.fold_in(seeds[5], 71), 0),
        "panel_order": draw_panel_order(jax.random.fold_in(seeds[5], 71), 0),
    }


def reference(x_window, square_rows, block_rank, block_count, panel_order):
    all_blocks = TILE_COLS * N_COL
    counts = jnp.repeat(jnp.repeat(block_count, SLAB_ROWS, axis=0), TILE_COLS, axis=1)
    live = (block_rank < counts).astype(jnp.float32)
    row_count = N_ROW * SLAB_ROWS
    shaped = x_window.reshape(row_count, BLOCK_WIDTH, all_blocks, BLOCK_WIDTH)
    filtered = (shaped * live[:, None, :, None]).reshape(x_window.shape)
    product = jnp.zeros(x_window.shape, jnp.float32)
    for step in range(ROUNDS):
        window = panel_order[step].astype(jnp.int32)
        column = ((window * all_blocks) // (WIN_ROWS * N_ROW)).astype(jnp.int32)
        left = lax.dynamic_slice_in_dim(filtered, column * BLOCK_WIDTH, BLOCK_WIDTH, 1)
        right = lax.dynamic_slice_in_dim(square_rows, window * BLOCK_WIDTH, BLOCK_WIDTH, 0)
        product = product + jnp.dot(left, right, preferred_element_type=jnp.float32, precision=lax.Precision.HIGHEST)
    update = 1.5 * filtered - 0.5 * product
    update = (update.reshape(row_count, BLOCK_WIDTH, all_blocks, BLOCK_WIDTH) * live[:, None, :, None]).reshape(x_window.shape)
    return update, jnp.sum(update * update)
```

```python
import functools

import jax
import jax.numpy as jnp
from jax import lax
from jax.experimental import pallas as pl
from jax.experimental.pallas import tpu as pltpu
from jax.sharding import PartitionSpec as P

BLOCK = 128
HALF = 64
TILE_COLS = 15
ROUNDS = 3
UNITS = TILE_COLS * ROUNDS
CHIPS = 6
N_X, N_Y, N_Z = 4, 8, 12
LAST = 23
PIECE = BLOCK // N_Y
LAG = 4
SIB_LAG = 2
PHASES = (9, 15, 24, 30, 38)
MM_FIRST = PHASES[-1]
STEPS = UNITS + (CHIPS - 1) * LAG + SIB_LAG
MESH = pl.DeviceIdType.MESH


def kernel(
    panel, rank, count, x_hbm, sq_hbm, out_hbm, total,
    xv, win, up, down, panels, out, lsrc, pa, pb, pc, pd, pe, ph, left,
    acc, qs, qz, qy, qx,
    load_sem, win_sem, wsend, wrecv,
    up_s, up_r, dn_s, dn_r, sib_s, sib_r,
    p1_s, p1_r, p2_s, p2_r, p3_s, p3_r, p4_s, p4_r, p5_s, p5_r,
    qs_s, qs_r, qz_s, qz_r, qy_s, qy_r, qx_s, qx_r,
):
    row = lax.axis_index("row")
    col = lax.axis_index("col")
    chip, core = row // 2, row % 2
    zh = col % 2
    y = (col // 2) % N_Y
    x = col // (2 * N_Y)
    z = zh * CHIPS + chip

    def at_z(zz):
        return ((zz % CHIPS) * 2 + core, (x * N_Y + y) * 2 + zz // CHIPS)

    def at_y(yy):
        return (row, (x * N_Y + yy) * 2 + zh)

    def at_x(xx):
        return (row, (xx * N_Y + y) * 2 + zh)

    sibling = (chip * 2 + 1 - core, col)
    z_peers = [at_z(lax.rem(z + d, N_Z)) for d in range(1, N_Z)]
    y_peers = [at_y(lax.rem(y + d, N_Y)) for d in range(1, N_Y)]
    x_peers = [at_x(lax.rem(x + d, N_X)) for d in range(1, N_X)]
    other_zh = (row, (x * N_Y + y) * 2 + 1 - zh)
    above = (row + 2, col)
    below = (row - 2, col)

    def remote(src, dst, send, recv, device):
        return pltpu.make_async_remote_copy(
            src_ref=src, dst_ref=dst, send_sem=send, recv_sem=recv,
            device_id=device, device_id_type=MESH,
        )

    barrier = pltpu.get_barrier_semaphore()
    everyone = [sibling] + z_peers + y_peers + x_peers
    for peer in everyone:
        pl.semaphore_signal(barrier, inc=1, device_id=peer, device_id_type=MESH)

    x_load = pltpu.make_async_copy(x_hbm, xv, load_sem.at[0])
    x_load.start()
    cuts = ((0, 3 * BLOCK), (3 * BLOCK, 12 * BLOCK))
    win_loads, win_sends = [], []
    for part, (first, width) in enumerate(cuts):
        for w in range(2):
            win_loads.append(pltpu.make_async_copy(
                sq_hbm.at[pl.ds(w * BLOCK + core * HALF, HALF), pl.ds(first, width)],
                win.at[2 * core + w, :, pl.ds(first, width)],
                win_sem.at[part, w],
            ))
            win_sends.append(remote(
                sq_hbm.at[pl.ds(w * BLOCK + (1 - core) * HALF, HALF), pl.ds(first, width)],
                win.at[2 * core + w, :, pl.ds(first, width)],
                wsend.at[part, w], wrecv.at[part, w], sibling,
            ))

    def win_arrival(part, w):
        first, width = cuts[part]
        dst = win.at[2 * (1 - core) + w, :, pl.ds(first, width)]
        return remote(dst, dst, wsend.at[part, w], wrecv.at[part, w], sibling)

    for copy in win_loads:
        copy.start()

    p0, p1, p2 = panel[0], panel[1], panel[2]
    q0 = jnp.where(p0 == LAST, p1, p0)
    q1 = jnp.where(p2 == LAST, p1, p2)
    q = (q0, q1, jnp.int32(LAST))
    owner_col = [(8 * w) // 3 for w in q]

    cand = (3 * col + 7) // 8
    place = jnp.minimum(40 * cand - TILE_COLS * col, TILE_COLS - 1)
    x_load.wait()
    cand_live = rank[0, place] < count[0, 0]
    lsrc[...] = jnp.where(
        cand_live, xv[:, pl.ds(pl.multiple_of(place * BLOCK, BLOCK), BLOCK)], 0.0
    )

    pl.semaphore_wait(barrier, len(everyone))

    for copy in win_sends:
        copy.start()

    def p1_copy(d):
        to = lax.rem(y + d, N_Y)
        return remote(
            lsrc.at[pl.ds(to * PIECE, PIECE)], pa.at[y], p1_s.at[d - 1], p1_r.at[d - 1], at_y(to)
        )

    def p1_wait(d):
        frm = lax.rem(y + N_Y - d, N_Y)
        return remote(pa.at[frm], pa.at[frm], p1_s.at[d - 1], p1_r.at[d - 1], at_y(frm))

    for d in range(1, N_Y):
        p1_copy(d).start()
    pa[y] = lsrc[pl.ds(pl.multiple_of(y * PIECE, PIECE), PIECE), :]

    def p2_copy(t):
        return remote(pb.at[t], pc.at[x], p2_s.at[t], p2_r.at[x], at_x(t))

    def p2_wait(frm):
        return remote(pc.at[frm], pc.at[frm], p2_s.at[0], p2_r.at[frm], at_x(frm))

    def p3_copy():
        return remote(pd, pe, p3_s.at[0], p3_r.at[0], other_zh)

    def p4_slot(t):
        return ph.at[:, pl.ds(pl.multiple_of(t * BLOCK, BLOCK), BLOCK)]

    def p4_copy(d):
        return remote(
            p4_slot(x), p4_slot(x), p4_s.at[d - 1], p4_r.at[d - 1], at_x(lax.rem(x + d, N_X))
        )

    def p4_wait(d):
        frm = lax.rem(x + N_X - d, N_X)
        return remote(p4_slot(frm), p4_slot(frm), p4_s.at[d - 1], p4_r.at[d - 1], at_x(frm))

    def left_rows(yy):
        return left.at[pl.ds(pl.multiple_of(yy * PIECE, PIECE), PIECE), :]

    def p5_copy(d):
        return remote(
            ph, left_rows(y), p5_s.at[d - 1], p5_r.at[d - 1], at_y(lax.rem(y + d, N_Y))
        )

    def p5_wait(d):
        frm = lax.rem(y + N_Y - d, N_Y)
        return remote(left_rows(frm), left_rows(frm), p5_s.at[d - 1], p5_r.at[d - 1], at_y(frm))

    def phase_1_to_2():
        for d in range(1, N_Y):
            p1_wait(d).wait_recv()
        for t in range(ROUNDS):
            pb[t] = pa[(owner_col[t] // 2) % N_Y]
        for t in range(ROUNDS):
            @pl.when(x != t)
            def _(t=t):
                p2_copy(t).start()

            @pl.when(x == t)
            def _(t=t):
                pc[t] = pb[t]

    my_owner = jnp.where(x == 0, owner_col[0], jnp.where(x == 1, owner_col[1], owner_col[2]))

    def phase_2_to_3():
        @pl.when(x < ROUNDS)
        def _():
            for frm in range(N_X):
                @pl.when(x != frm)
                def _(frm=frm):
                    p2_wait(frm).wait_recv()
            pd[...] = pc[my_owner // (2 * N_Y)]
            p3_copy().start()

    def phase_3_to_4():
        @pl.when(x < ROUNDS)
        def _():
            p3_copy().wait_recv()
            mine = jnp.where(my_owner % 2 == zh, pd[...], pe[...])
            ph[:, pl.ds(pl.multiple_of(x * BLOCK, BLOCK), BLOCK)] = mine
            for d in range(1, N_X):
                p4_copy(d).start()

    def phase_4_to_5():
        for d in range(1, N_X):
            @pl.when(lax.rem(x + N_X - d, N_X) < ROUNDS)
            def _(d=d):
                p4_wait(d).wait_recv()
        left[pl.ds(pl.multiple_of(y * PIECE, PIECE), PIECE), :] = ph[...]
        for d in range(1, N_Y):
            p5_copy(d).start()

    def phase_5_end():
        for d in range(1, N_Y):
            p5_wait(d).wait_recv()

    def up_copy(u):
        return remote(up.at[u], up.at[u], up_s.at[u], up_r.at[u], above)

    def down_copy(u):
        return remote(down.at[u], down.at[u], dn_s.at[u], dn_r.at[u], below)

    def sib_slot(u, half):
        return panels.at[u, pl.ds(pl.multiple_of(half * HALF, HALF), HALF), :]

    def sib_copy(u):
        return remote(sib_slot(u, core), sib_slot(u, core), sib_s.at[u], sib_r.at[u], sibling)

    def sib_wait(u):
        return remote(
            sib_slot(u, 1 - core), sib_slot(u, 1 - core), sib_s.at[u], sib_r.at[u], sibling
        )

    def window_of(t):
        return jnp.where(t == 0, q[0], jnp.where(t == 1, q[1], q[2]))

    def inject(buf, u):
        j, t = u // ROUNDS, u % ROUNDS
        w = window_of(t)
        cols = pl.ds(pl.multiple_of(j * BLOCK, BLOCK), BLOCK)
        value = buf[u]
        for k in range(4):
            value = jnp.where(w == 4 * chip + k, win[k, :, cols], value)
        buf[u] = value

    far = jnp.maximum(chip, CHIPS - 1 - chip)
    acc[...] = jnp.zeros_like(acc)

    for w in range(2):
        win_loads[w].wait()
        win_arrival(0, w).wait_recv()

    def multiply(j):
        for t in range(ROUNDS):
            sib_wait(j * ROUNDS + t).wait_recv()
        right = panels[pl.ds(j * ROUNDS, ROUNDS)].reshape(ROUNDS * BLOCK, BLOCK)
        product = jnp.dot(
            left[...], right, preferred_element_type=jnp.float32, precision=lax.Precision.HIGHEST
        )
        cols = pl.ds(pl.multiple_of(j * BLOCK, BLOCK), BLOCK)
        live = rank[0, j] < count[0, 0]
        update = jnp.where(live, 1.5 * xv[:, cols] - 0.5 * product, 0.0)
        out[:, cols] = update
        acc[...] += jnp.sum((update * update).reshape(BLOCK // 8, 8, BLOCK), axis=0)

    def step(s, j):
        @pl.when(s == 9)
        def _():
            for w in range(2):
                win_loads[2 + w].wait()
                win_arrival(1, w).wait_recv()

        u = s - chip * LAG

        @pl.when((u >= 0) & (u < UNITS) & (lax.rem(u + ROUNDS * 40, ROUNDS) < 2))
        def _():
            @pl.when(chip > 0)
            def _():
                up_copy(u).wait_recv()

            inject(up, u)

            @pl.when(chip < CHIPS - 1)
            def _():
                up_copy(u).start()

        d = s - (CHIPS - 1 - chip) * LAG

        @pl.when((d >= 0) & (d < UNITS))
        def _():
            @pl.when(chip < CHIPS - 1)
            def _():
                down_copy(d).wait_recv()

            inject(down, d)

            @pl.when(chip > 0)
            def _():
                down_copy(d).start()

        f = s - far * LAG

        @pl.when((f >= 0) & (f < UNITS))
        def _():
            t = f % ROUNDS
            from_up = window_of(t) // 4 < chip
            panels[f, pl.ds(pl.multiple_of(core * HALF, HALF), HALF), :] = jnp.where(
                from_up, up[f], down[f]
            )
            sib_copy(f).start()

        for at, phase in zip(
            PHASES, (phase_1_to_2, phase_2_to_3, phase_3_to_4, phase_4_to_5, phase_5_end)
        ):
            pl.when(s == at)(phase)

        ready = (
            (j < TILE_COLS)
            & (s >= MM_FIRST + 2 * j)
            & (s >= ROUNDS * j + ROUNDS - 1 + far * LAG + SIB_LAG)
        )

        @pl.when(ready)
        def _():
            multiply(j)

        return j + ready.astype(jnp.int32)

    lax.fori_loop(0, STEPS, step, jnp.int32(0))

    store = pltpu.make_async_copy(out, out_hbm, load_sem.at[1])
    store.start()

    sib_sum = remote(acc, qs.at[0], qs_s.at[0], qs_r.at[0], sibling)
    sib_sum.start()

    for copy in win_sends:
        copy.wait_send()
    for d in range(1, N_Y):
        p1_copy(d).wait_send()
        p5_copy(d).wait_send()
    for t in range(ROUNDS):
        @pl.when(x != t)
        def _(t=t):
            p2_copy(t).wait_send()

    @pl.when(x < ROUNDS)
    def _():
        p3_copy().wait_send()
        for d in range(1, N_X):
            p4_copy(d).wait_send()

    sib_sum.wait()
    qz[z] = acc[...] + qs[0]
    z_sums = [
        remote(qz.at[z], qz.at[z], qz_s.at[d - 1], qz_r.at[d - 1], peer)
        for d, peer in enumerate(z_peers, 1)
    ]
    for copy in z_sums:
        copy.start()

    def drain(u, carry):
        sib_copy(u).wait_send()

        @pl.when((chip < CHIPS - 1) & (u % ROUNDS < 2))
        def _():
            up_copy(u).wait_send()

        @pl.when(chip > 0)
        def _():
            down_copy(u).wait_send()

        return carry

    lax.fori_loop(0, UNITS, drain, 0)

    for d in range(1, N_Z):
        frm = lax.rem(z + N_Z - d, N_Z)
        remote(qz.at[frm], qz.at[frm], qz_s.at[d - 1], qz_r.at[d - 1], at_z(frm)).wait_recv()
    qy[y] = jnp.sum(qz[...], axis=0)
    y_sums = [
        remote(qy.at[y], qy.at[y], qy_s.at[d - 1], qy_r.at[d - 1], peer)
        for d, peer in enumerate(y_peers, 1)
    ]
    for copy in y_sums:
        copy.start()
    for d in range(1, N_Y):
        frm = lax.rem(y + N_Y - d, N_Y)
        remote(qy.at[frm], qy.at[frm], qy_s.at[d - 1], qy_r.at[d - 1], at_y(frm)).wait_recv()
    qx[x] = jnp.sum(qy[...], axis=0)
    x_sums = [
        remote(qx.at[x], qx.at[x], qx_s.at[d - 1], qx_r.at[d - 1], peer)
        for d, peer in enumerate(x_peers, 1)
    ]
    for copy in x_sums:
        copy.start()
    for d in range(1, N_X):
        frm = lax.rem(x + N_X - d, N_X)
        remote(qx.at[frm], qx.at[frm], qx_s.at[d - 1], qx_r.at[d - 1], at_x(frm)).wait_recv()
    total[0, 0] = jnp.sum(jnp.sum(qx[...], axis=0))
    for copy in z_sums + y_sums + x_sums:
        copy.wait_send()
    store.wait()


def on_device(x_window, square_rows, block_rank, block_count, panel_order):
    width = TILE_COLS * BLOCK
    vmem = lambda *shape: pltpu.VMEM(shape, jnp.float32)
    dma = lambda *shape: pltpu.SemaphoreType.DMA(shape)
    updated, total = pl.pallas_call(
        kernel,
        out_shape=(
            jax.ShapeDtypeStruct((BLOCK, width), jnp.float32),
            jax.ShapeDtypeStruct((1, 1), jnp.float32),
        ),
        in_specs=[pl.BlockSpec(memory_space=pltpu.SMEM)] * 3
        + [pl.BlockSpec(memory_space=pl.ANY)] * 2,
        out_specs=(
            pl.BlockSpec(memory_space=pl.ANY),
            pl.BlockSpec(memory_space=pltpu.SMEM),
        ),
        scratch_shapes=[
            vmem(BLOCK, width),
            vmem(4, HALF, width),
            vmem(UNITS, HALF, BLOCK),
            vmem(UNITS, HALF, BLOCK),
            vmem(UNITS, BLOCK, BLOCK),
            vmem(BLOCK, width),
            vmem(BLOCK, BLOCK),
            vmem(N_Y, PIECE, BLOCK),
            vmem(ROUNDS, PIECE, BLOCK),
            vmem(N_X, PIECE, BLOCK),
            vmem(PIECE, BLOCK),
            vmem(PIECE, BLOCK),
            vmem(PIECE, ROUNDS * BLOCK),
            vmem(BLOCK, ROUNDS * BLOCK),
            vmem(8, BLOCK),
            vmem(1, 8, BLOCK),
            vmem(N_Z, 8, BLOCK),
            vmem(N_Y, 8, BLOCK),
            vmem(N_X, 8, BLOCK),
            dma(2), dma(2, 2), dma(2, 2), dma(2, 2),
            dma(UNITS), dma(UNITS), dma(UNITS), dma(UNITS), dma(UNITS), dma(UNITS),
            dma(N_Y - 1), dma(N_Y - 1), dma(ROUNDS), dma(N_X), dma(1), dma(1),
            dma(N_X - 1), dma(N_X - 1), dma(N_Y - 1), dma(N_Y - 1),
            dma(1), dma(1), dma(N_Z - 1), dma(N_Z - 1),
            dma(N_Y - 1), dma(N_Y - 1), dma(N_X - 1), dma(N_X - 1),
        ],
        compiler_params=pltpu.CompilerParams(
            collective_id=0, has_side_effects=True, vmem_limit_bytes=40 << 20
        ),
        name="sign_window",
    )(panel_order, block_rank, block_count, x_window, square_rows)
    return updated, total[0, 0]


def solution(mesh):
    return jax.shard_map(
        on_device,
        mesh=mesh,
        in_specs=(P("row", "col"), P("row", "col"), P("row", "col"), P("row", "col"), P()),
        out_specs=(P("row", "col"), P()),
        check_vma=False,
    )
```

```python
import functools

import jax
import jax.numpy as jnp
from jax import lax
from jax.experimental import pallas as pl
from jax.experimental.pallas import tpu as pltpu
from jax.sharding import PartitionSpec as P

BLOCK = 128
HALF = 64
TILE_COLS = 15
ROUNDS = 3
UNITS = TILE_COLS * ROUNDS
CHIPS = 6
N_X, N_Y, N_Z = 4, 8, 12
LAST = 23
PIECE = BLOCK // N_Y
FAR_Z = (6, 5, 7, 4, 8, 3, 9, 2, 10, 1, 11)
FAR_Y = (4, 3, 5, 2, 6, 1, 7)
FAR_X = (2, 1, 3)
LAG = 6
SIB_LAG = 2
PHASES = (12, 20, 30, 37, 44)
MM_FIRST = PHASES[-1]
WRAPS = 5
WRAP_FIRST = 7
DOWN_LAST = TILE_COLS - WRAPS
TRIPLES = WRAP_FIRST + WRAPS
SLOTS = 3 * TRIPLES + 2 * (TILE_COLS - TRIPLES)
RELAY_STEP = 18
STEPS = SLOTS + (CHIPS - 1) * LAG + SIB_LAG
MESH = pl.DeviceIdType.MESH


def kernel(
    panel, rank, count, x_hbm, sq_hbm, out_hbm, total,
    xv, win, up, down, relay, panels, out, lsrc, pa, pb, pc, pd, pe, ph, left,
    acc, qs, qz, qy, qx,
    load_sem, win_sem, wsend, wrecv,
    up_s, up_r, dn_s, dn_r, rl_s, rl_r, wr_s, sib_s, sib_r,
    p1_s, p1_r, p2_s, p2_r, p3_s, p3_r, p4_s, p4_r, p5_s, p5_r,
    qs_s, qs_r, qz_s, qz_r, qy_s, qy_r, qx_s, qx_r,
):
    row = lax.axis_index("row")
    col = lax.axis_index("col")
    chip, core = row // 2, row % 2
    zh = col % 2
    y = (col // 2) % N_Y
    x = col // (2 * N_Y)
    z = zh * CHIPS + chip

    def at_z(zz):
        return ((zz % CHIPS) * 2 + core, (x * N_Y + y) * 2 + zz // CHIPS)

    def at_y(yy):
        return (row, (x * N_Y + yy) * 2 + zh)

    def at_x(xx):
        return (row, (xx * N_Y + y) * 2 + zh)

    sibling = (chip * 2 + 1 - core, col)
    z_peers = [at_z(lax.rem(z + d, N_Z)) for d in FAR_Z]
    y_peers = [at_y(lax.rem(y + d, N_Y)) for d in FAR_Y]
    x_peers = [at_x(lax.rem(x + d, N_X)) for d in FAR_X]
    other_zh = (row, (x * N_Y + y) * 2 + 1 - zh)
    above = (row + 2, col)
    below = (row - 2, col)

    def remote(src, dst, send, recv, device):
        return pltpu.make_async_remote_copy(
            src_ref=src, dst_ref=dst, send_sem=send, recv_sem=recv,
            device_id=device, device_id_type=MESH,
        )

    barrier = pltpu.get_barrier_semaphore()
    everyone = [sibling] + z_peers + y_peers + x_peers
    for peer in everyone:
        pl.semaphore_signal(barrier, inc=1, device_id=peer, device_id_type=MESH)

    x_load = pltpu.make_async_copy(x_hbm, xv, load_sem.at[0])
    x_load.start()
    cuts = ((0, 3 * BLOCK), (3 * BLOCK, 12 * BLOCK))
    win_loads, win_sends = [], []
    for part, (first, width) in enumerate(cuts):
        for w in range(2):
            win_loads.append(pltpu.make_async_copy(
                sq_hbm.at[pl.ds(w * BLOCK + core * HALF, HALF), pl.ds(first, width)],
                win.at[2 * core + w, :, pl.ds(first, width)],
                win_sem.at[part, w],
            ))
            win_sends.append(remote(
                sq_hbm.at[pl.ds(w * BLOCK + (1 - core) * HALF, HALF), pl.ds(first, width)],
                win.at[2 * core + w, :, pl.ds(first, width)],
                wsend.at[part, w], wrecv.at[part, w], sibling,
            ))

    def win_arrival(part, w):
        first, width = cuts[part]
        dst = win.at[2 * (1 - core) + w, :, pl.ds(first, width)]
        return remote(dst, dst, wsend.at[part, w], wrecv.at[part, w], sibling)

    for copy in win_loads:
        copy.start()

    p0, p1, p2 = panel[0], panel[1], panel[2]
    q0 = jnp.where(p0 == LAST, p1, p0)
    q1 = jnp.where(p2 == LAST, p1, p2)
    q = (q0, q1, jnp.int32(LAST))
    owner_col = [(8 * w) // 3 for w in q]

    cand = (3 * col + 7) // 8
    place = jnp.minimum(40 * cand - TILE_COLS * col, TILE_COLS - 1)
    x_load.wait()
    cand_live = rank[0, place] < count[0, 0]
    lsrc[...] = jnp.where(
        cand_live, xv[:, pl.ds(pl.multiple_of(place * BLOCK, BLOCK), BLOCK)], 0.0
    )

    pl.semaphore_wait(barrier, len(everyone))

    for copy in win_sends:
        copy.start()

    def p1_copy(d):
        to = lax.rem(y + d, N_Y)
        return remote(
            lsrc.at[pl.ds(to * PIECE, PIECE)], pa.at[y], p1_s.at[d - 1], p1_r.at[d - 1], at_y(to)
        )

    def p1_wait(d):
        frm = lax.rem(y + N_Y - d, N_Y)
        return remote(pa.at[frm], pa.at[frm], p1_s.at[d - 1], p1_r.at[d - 1], at_y(frm))

    for d in FAR_Y:
        p1_copy(d).start()
    pa[y] = lsrc[pl.ds(pl.multiple_of(y * PIECE, PIECE), PIECE), :]

    def p2_copy(t):
        return remote(pb.at[t], pc.at[x], p2_s.at[t], p2_r.at[x], at_x(t))

    def p2_wait(frm):
        return remote(pc.at[frm], pc.at[frm], p2_s.at[0], p2_r.at[frm], at_x(frm))

    def p3_copy():
        return remote(pd, pe, p3_s.at[0], p3_r.at[0], other_zh)

    def p4_slot(t):
        return ph.at[:, pl.ds(pl.multiple_of(t * BLOCK, BLOCK), BLOCK)]

    def p4_copy(d):
        return remote(
            p4_slot(x), p4_slot(x), p4_s.at[d - 1], p4_r.at[d - 1], at_x(lax.rem(x + d, N_X))
        )

    def p4_wait(d):
        frm = lax.rem(x + N_X - d, N_X)
        return remote(p4_slot(frm), p4_slot(frm), p4_s.at[d - 1], p4_r.at[d - 1], at_x(frm))

    def left_rows(yy):
        return left.at[pl.ds(pl.multiple_of(yy * PIECE, PIECE), PIECE), :]

    def p5_copy(d):
        return remote(
            ph, left_rows(y), p5_s.at[d - 1], p5_r.at[d - 1], at_y(lax.rem(y + d, N_Y))
        )

    def p5_wait(d):
        frm = lax.rem(y + N_Y - d, N_Y)
        return remote(left_rows(frm), left_rows(frm), p5_s.at[d - 1], p5_r.at[d - 1], at_y(frm))

    def phase_1_to_2():
        for d in range(1, N_Y):
            p1_wait(d).wait_recv()
        for t in range(ROUNDS):
            pb[t] = pa[(owner_col[t] // 2) % N_Y]
        for t in range(ROUNDS):
            @pl.when(x != t)
            def _(t=t):
                p2_copy(t).start()

            @pl.when(x == t)
            def _(t=t):
                pc[t] = pb[t]

    my_owner = jnp.where(x == 0, owner_col[0], jnp.where(x == 1, owner_col[1], owner_col[2]))

    def phase_2_to_3():
        @pl.when(x < ROUNDS)
        def _():
            for frm in range(N_X):
                @pl.when(x != frm)
                def _(frm=frm):
                    p2_wait(frm).wait_recv()
            pd[...] = pc[my_owner // (2 * N_Y)]
            p3_copy().start()

    def phase_3_to_4():
        @pl.when(x < ROUNDS)
        def _():
            p3_copy().wait_recv()
            mine = jnp.where(my_owner % 2 == zh, pd[...], pe[...])
            ph[:, pl.ds(pl.multiple_of(x * BLOCK, BLOCK), BLOCK)] = mine
            for d in range(1, N_X):
                p4_copy(d).start()

    def phase_4_to_5():
        for d in range(1, N_X):
            @pl.when(lax.rem(x + N_X - d, N_X) < ROUNDS)
            def _(d=d):
                p4_wait(d).wait_recv()
        left[pl.ds(pl.multiple_of(y * PIECE, PIECE), PIECE), :] = ph[...]
        for d in FAR_Y:
            p5_copy(d).start()

    def phase_5_end():
        for d in range(1, N_Y):
            p5_wait(d).wait_recv()

    def up_copy(u):
        return remote(up.at[u], up.at[u], up_s.at[u], up_r.at[u], above)

    def down_copy(u):
        return remote(down.at[u], down.at[u], dn_s.at[u], dn_r.at[u], below)

    def sib_slot(u, half):
        return panels.at[u, pl.ds(pl.multiple_of(half * HALF, HALF), HALF), :]

    def sib_copy(u):
        return remote(sib_slot(u, core), sib_slot(u, core), sib_s.at[u], sib_r.at[u], sibling)

    def sib_wait(u):
        return remote(
            sib_slot(u, 1 - core), sib_slot(u, 1 - core), sib_s.at[u], sib_r.at[u], sibling
        )

    def window_of(t):
        return jnp.where(t == 0, q[0], jnp.where(t == 1, q[1], q[2]))

    def slot_of(u):
        late = u - 3 * TRIPLES
        j = jnp.where(late < 0, u // 3, TRIPLES + jnp.maximum(late, 0) // 2)
        t = jnp.where(late < 0, u % 3, jnp.maximum(late, 0) % 2)
        return j, t

    def columns(j):
        return pl.ds(pl.multiple_of(j * BLOCK, BLOCK), BLOCK)

    def inject(buf, u):
        j, t = slot_of(u)
        w = window_of(t)
        value = buf[u]
        for k in range(4):
            value = jnp.where(w == 4 * chip + k, win[k, :, columns(j)], value)
        buf[u] = value

    def wrap_copy(n):
        return remote(
            win.at[3, :, pl.ds((DOWN_LAST + n) * BLOCK, BLOCK)], relay.at[n],
            wr_s.at[n], rl_r.at[n], at_z(lax.rem(z + 4, N_Z)),
        )

    def relay_copy(n):
        slot = 3 * (WRAP_FIRST + n) + 2
        return remote(
            relay.at[n], up.at[slot], rl_s.at[n], up_r.at[slot], at_z(lax.rem(z + 3, N_Z))
        )

    far = jnp.maximum(chip, CHIPS - 1 - chip)
    acc[...] = jnp.zeros_like(acc)

    for w in range(2):
        win_loads[w].wait()
        win_arrival(0, w).wait_recv()

    def multiply(j):
        for t in range(ROUNDS):
            sib_wait(j * ROUNDS + t).wait_recv()
        right = panels[pl.ds(j * ROUNDS, ROUNDS)].reshape(ROUNDS * BLOCK, BLOCK)
        product = jnp.dot(
            left[...], right, preferred_element_type=jnp.float32, precision=lax.Precision.HIGHEST
        )
        cols = pl.ds(pl.multiple_of(j * BLOCK, BLOCK), BLOCK)
        live = rank[0, j] < count[0, 0]
        update = jnp.where(live, 1.5 * xv[:, cols] - 0.5 * product, 0.0)
        out[:, cols] = update
        acc[...] += jnp.sum((update * update).reshape(BLOCK // 8, 8, BLOCK), axis=0)

    def step(s, j):
        @pl.when(s == 9)
        def _():
            for w in range(2):
                win_loads[2 + w].wait()
                win_arrival(1, w).wait_recv()

        @pl.when((s == 10) & (chip == CHIPS - 1))
        def _():
            for n in range(WRAPS):
                wrap_copy(n).start()

        for n in range(WRAPS):
            @pl.when((s == RELAY_STEP + 2 * n) & (chip == 3))
            def _(n=n):
                remote(
                    relay.at[n], relay.at[n], wr_s.at[n], rl_r.at[n], at_z(lax.rem(z + 8, N_Z))
                ).wait_recv()
                relay_copy(n).start()

        u = s - chip * LAG
        uj, ut = slot_of(jnp.clip(u, 0, SLOTS - 1))

        @pl.when((u >= 0) & (u < SLOTS) & (ut < 2))
        def _():
            @pl.when(chip > 0)
            def _():
                up_copy(u).wait_recv()

            inject(up, u)

            @pl.when(chip < CHIPS - 1)
            def _():
                up_copy(u).start()

        @pl.when((u >= 0) & (u < SLOTS) & (ut == 2) & (uj >= WRAP_FIRST) & (chip < CHIPS - 1))
        def _():
            up_copy(u).wait_recv()

            @pl.when(chip < CHIPS - 2)
            def _():
                up_copy(u).start()

        d = s - (CHIPS - 1 - chip) * LAG
        dj, dt = slot_of(jnp.clip(d, 0, SLOTS - 1))

        @pl.when((d >= 0) & (d < SLOTS) & ((dt < 2) | (dj < DOWN_LAST)))
        def _():
            @pl.when(chip < CHIPS - 1)
            def _():
                down_copy(d).wait_recv()

            inject(down, d)

            @pl.when(chip > 0)
            def _():
                down_copy(d).start()

        f = s - far * LAG

        fj, ft = slot_of(jnp.clip(f, 0, SLOTS - 1))

        def finish(j, t, value):
            unit = ROUNDS * j + t
            panels[unit, pl.ds(pl.multiple_of(core * HALF, HALF), HALF), :] = value
            sib_copy(unit).start()

        @pl.when((f >= 0) & (f < SLOTS) & ((ft < 2) | (fj < DOWN_LAST)))
        def _():
            finish(fj, ft, jnp.where(window_of(ft) // 4 < chip, up[f], down[f]))

        wraps = (f >= 0) & (f < SLOTS) & (ft == 2) & (fj >= WRAP_FIRST)
        wrapped = fj + DOWN_LAST - WRAP_FIRST

        @pl.when(wraps & (chip < CHIPS - 1))
        def _():
            finish(wrapped, 2, up[f])

        @pl.when(wraps & (chip == CHIPS - 1))
        def _():
            finish(wrapped, 2, win[3, :, columns(wrapped)])

        for at, phase in zip(
            PHASES, (phase_1_to_2, phase_2_to_3, phase_3_to_4, phase_4_to_5, phase_5_end)
        ):
            pl.when(s == at)(phase)

        ready = (
            (j < TILE_COLS)
            & (s >= MM_FIRST + 2 * j)
            & (s >= jnp.minimum(3 * j + 2, 2 * j + TRIPLES + 1) + far * LAG + SIB_LAG)
        )

        @pl.when(ready)
        def _():
            multiply(j)

        return j + ready.astype(jnp.int32)

    lax.fori_loop(0, STEPS, step, jnp.int32(0))

    store = pltpu.make_async_copy(out, out_hbm, load_sem.at[1])
    store.start()

    sib_sum = remote(acc, qs.at[0], qs_s.at[0], qs_r.at[0], sibling)
    sib_sum.start()

    for copy in win_sends:
        copy.wait_send()
    for d in range(1, N_Y):
        p1_copy(d).wait_send()
        p5_copy(d).wait_send()
    for t in range(ROUNDS):
        @pl.when(x != t)
        def _(t=t):
            p2_copy(t).wait_send()

    @pl.when(x < ROUNDS)
    def _():
        p3_copy().wait_send()
        for d in range(1, N_X):
            p4_copy(d).wait_send()

    sib_sum.wait()
    qz[z] = acc[...] + qs[0]
    z_sums = [
        remote(qz.at[z], qz.at[z], qz_s.at[d - 1], qz_r.at[d - 1], peer)
        for d, peer in zip(FAR_Z, z_peers)
    ]
    for copy in z_sums:
        copy.start()

    def drain(u, carry):
        j, t = slot_of(u)

        @pl.when(
            (chip < CHIPS - 1) & (t < 2) | (chip < CHIPS - 2) & (t == 2) & (j >= WRAP_FIRST)
        )
        def _():
            up_copy(u).wait_send()

        @pl.when((chip > 0) & ((t < 2) | (j < DOWN_LAST)))
        def _():
            down_copy(u).wait_send()

        return carry

    lax.fori_loop(0, SLOTS, drain, 0)

    def drain_sib(u, carry):
        sib_copy(u).wait_send()
        return carry

    lax.fori_loop(0, UNITS, drain_sib, 0)
    for n in range(WRAPS):
        @pl.when(chip == CHIPS - 1)
        def _(n=n):
            wrap_copy(n).wait_send()

        @pl.when(chip == 3)
        def _(n=n):
            relay_copy(n).wait_send()

    for d in range(1, N_Z):
        frm = lax.rem(z + N_Z - d, N_Z)
        remote(qz.at[frm], qz.at[frm], qz_s.at[d - 1], qz_r.at[d - 1], at_z(frm)).wait_recv()
    qy[y] = jnp.sum(qz[...], axis=0)
    y_sums = [
        remote(qy.at[y], qy.at[y], qy_s.at[d - 1], qy_r.at[d - 1], peer)
        for d, peer in zip(FAR_Y, y_peers)
    ]
    for copy in y_sums:
        copy.start()
    for d in range(1, N_Y):
        frm = lax.rem(y + N_Y - d, N_Y)
        remote(qy.at[frm], qy.at[frm], qy_s.at[d - 1], qy_r.at[d - 1], at_y(frm)).wait_recv()
    qx[x] = jnp.sum(qy[...], axis=0)
    x_sums = [
        remote(qx.at[x], qx.at[x], qx_s.at[d - 1], qx_r.at[d - 1], peer)
        for d, peer in zip(FAR_X, x_peers)
    ]
    for copy in x_sums:
        copy.start()
    for d in range(1, N_X):
        frm = lax.rem(x + N_X - d, N_X)
        remote(qx.at[frm], qx.at[frm], qx_s.at[d - 1], qx_r.at[d - 1], at_x(frm)).wait_recv()
    total[0, 0] = jnp.sum(jnp.sum(qx[...], axis=0))
    for copy in z_sums + y_sums + x_sums:
        copy.wait_send()
    store.wait()


def on_device(x_window, square_rows, block_rank, block_count, panel_order):
    width = TILE_COLS * BLOCK
    vmem = lambda *shape: pltpu.VMEM(shape, jnp.float32)
    dma = lambda *shape: pltpu.SemaphoreType.DMA(shape)
    updated, total = pl.pallas_call(
        kernel,
        out_shape=(
            jax.ShapeDtypeStruct((BLOCK, width), jnp.float32),
            jax.ShapeDtypeStruct((1, 1), jnp.float32),
        ),
        in_specs=[pl.BlockSpec(memory_space=pltpu.SMEM)] * 3
        + [pl.BlockSpec(memory_space=pl.ANY)] * 2,
        out_specs=(
            pl.BlockSpec(memory_space=pl.ANY),
            pl.BlockSpec(memory_space=pltpu.SMEM),
        ),
        scratch_shapes=[
            vmem(BLOCK, width),
            vmem(4, HALF, width),
            vmem(SLOTS, HALF, BLOCK),
            vmem(SLOTS, HALF, BLOCK),
            vmem(WRAPS, HALF, BLOCK),
            vmem(UNITS, BLOCK, BLOCK),
            vmem(BLOCK, width),
            vmem(BLOCK, BLOCK),
            vmem(N_Y, PIECE, BLOCK),
            vmem(ROUNDS, PIECE, BLOCK),
            vmem(N_X, PIECE, BLOCK),
            vmem(PIECE, BLOCK),
            vmem(PIECE, BLOCK),
            vmem(PIECE, ROUNDS * BLOCK),
            vmem(BLOCK, ROUNDS * BLOCK),
            vmem(8, BLOCK),
            vmem(1, 8, BLOCK),
            vmem(N_Z, 8, BLOCK),
            vmem(N_Y, 8, BLOCK),
            vmem(N_X, 8, BLOCK),
            dma(2), dma(2, 2), dma(2, 2), dma(2, 2),
            dma(SLOTS), dma(SLOTS), dma(SLOTS), dma(SLOTS),
            dma(WRAPS), dma(WRAPS), dma(WRAPS), dma(UNITS), dma(UNITS),
            dma(N_Y - 1), dma(N_Y - 1), dma(ROUNDS), dma(N_X), dma(1), dma(1),
            dma(N_X - 1), dma(N_X - 1), dma(N_Y - 1), dma(N_Y - 1),
            dma(1), dma(1), dma(N_Z - 1), dma(N_Z - 1),
            dma(N_Y - 1), dma(N_Y - 1), dma(N_X - 1), dma(N_X - 1),
        ],
        compiler_params=pltpu.CompilerParams(
            collective_id=0, has_side_effects=True, vmem_limit_bytes=62 << 20
        ),
        name="sign_window",
    )(panel_order, block_rank, block_count, x_window, square_rows)
    return updated, total[0, 0]


def solution(mesh):
    return jax.shard_map(
        on_device,
        mesh=mesh,
        in_specs=(P("row", "col"), P("row", "col"), P("row", "col"), P("row", "col"), P()),
        out_specs=(P("row", "col"), P()),
        check_vma=False,
    )
```

```python
import functools

import jax
import jax.numpy as jnp
from jax import lax
from jax.experimental import pallas as pl
from jax.experimental.pallas import tpu as pltpu
from jax.sharding import PartitionSpec as P

BLOCK = 128
HALF = 64
TILE_COLS = 15
ROUNDS = 3
SUB = 1
PART = HALF // SUB
UNITS = TILE_COLS * ROUNDS
CHIPS = 6
N_X, N_Y, N_Z = 4, 8, 12
LAST = 23
PIECE = BLOCK // N_Y
FAR_Z = (6, 5, 7, 4, 8, 3, 9, 2, 10, 1, 11)
FAR_Y = (4, 3, 5, 2, 6, 1, 7)
FAR_X = (2, 1, 3)
LAG = 6
SIB_LAG = 2
PHASES = (12, 20, 30, 37, 44)
MM_FIRST = PHASES[-1]
WRAPS = 5
WRAP_FIRST = 7
DOWN_LAST = TILE_COLS - WRAPS
TRIPLES = WRAP_FIRST + WRAPS
SLOTS = 3 * TRIPLES + 2 * (TILE_COLS - TRIPLES)
RELAY_STEP = 22
STEPS = SLOTS + (CHIPS - 1) * LAG + SIB_LAG
MESH = pl.DeviceIdType.MESH


def kernel(
    panel_hbm, rank_hbm, count_hbm, x_hbm, sq_hbm, out_hbm, total,
    panel, rank, count,
    xv, win, up, down, relay, panels, out, lsrc, pa, pb, pc, pd, pe, ph, left, left_high, left_low,
    acc, qs, qz, qy, qx,
    small_sem, load_sem, win_sem, wsend, wrecv,
    up_s, up_r, dn_s, dn_r, rl_s, rl_r, wr_s, sib_s, sib_r,
    p1_s, p1_r, p2_s, p2_r, p3_s, p3_r, p4_s, p4_r, p5_s, p5_r,
    qs_s, qs_r, qz_s, qz_r, qy_s, qy_r, qx_s, qx_r,
):
    row = lax.axis_index("row")
    col = lax.axis_index("col")
    chip, core = row // 2, row % 2
    zh = col % 2
    y = (col // 2) % N_Y
    x = col // (2 * N_Y)
    z = zh * CHIPS + chip

    def at_z(zz):
        return ((zz % CHIPS) * 2 + core, (x * N_Y + y) * 2 + zz // CHIPS)

    def at_y(yy):
        return (row, (x * N_Y + yy) * 2 + zh)

    def at_x(xx):
        return (row, (xx * N_Y + y) * 2 + zh)

    sibling = (chip * 2 + 1 - core, col)
    z_peers = [at_z(lax.rem(z + d, N_Z)) for d in FAR_Z]
    y_peers = [at_y(lax.rem(y + d, N_Y)) for d in FAR_Y]
    x_peers = [at_x(lax.rem(x + d, N_X)) for d in FAR_X]
    other_zh = (row, (x * N_Y + y) * 2 + 1 - zh)
    above = (row + 2, col)
    below = (row - 2, col)

    def remote(src, dst, send, recv, device):
        return pltpu.make_async_remote_copy(
            src_ref=src, dst_ref=dst, send_sem=send, recv_sem=recv,
            device_id=device, device_id_type=MESH,
        )

    small_loads = [
        pltpu.make_async_copy(src, dst, small_sem.at[n])
        for n, (src, dst) in enumerate(((panel_hbm, panel), (rank_hbm, rank), (count_hbm, count)))
    ]
    for copy in small_loads:
        copy.start()

    barrier = pltpu.get_barrier_semaphore()
    everyone = [sibling] + z_peers[::-1] + y_peers + x_peers
    for peer in everyone:
        pl.semaphore_signal(barrier, inc=1, device_id=peer, device_id_type=MESH)

    x_load = pltpu.make_async_copy(x_hbm, xv, load_sem.at[0])
    cuts = ((0, 3 * BLOCK), (3 * BLOCK, 12 * BLOCK))
    win_loads, win_sends = [], []
    for part, (first, width) in enumerate(cuts):
        for w in range(2):
            win_loads.append(pltpu.make_async_copy(
                sq_hbm.at[pl.ds(w * BLOCK + core * HALF, HALF), pl.ds(first, width)],
                win.at[2 * core + w, :, pl.ds(first, width)],
                win_sem.at[part, w],
            ))
            win_sends.append(remote(
                sq_hbm.at[pl.ds(w * BLOCK + (1 - core) * HALF, HALF), pl.ds(first, width)],
                win.at[2 * core + w, :, pl.ds(first, width)],
                wsend.at[part, w], wrecv.at[part, w], sibling,
            ))

    def win_arrival(part, w):
        first, width = cuts[part]
        dst = win.at[2 * (1 - core) + w, :, pl.ds(first, width)]
        return remote(dst, dst, wsend.at[part, w], wrecv.at[part, w], sibling)

    for copy in win_loads[:2]:
        copy.start()
    x_load.start()
    for copy in win_loads[2:]:
        copy.start()

    pl.semaphore_wait(barrier, len(everyone))

    for copy in win_sends:
        copy.start()

    for copy in small_loads:
        copy.wait()

    p0, p1, p2 = panel[0], panel[1], panel[2]
    q0 = jnp.where(p0 == LAST, p1, p0)
    q1 = jnp.where(p2 == LAST, p1, p2)
    q = (q0, q1, jnp.int32(LAST))
    owner_col = [(8 * w) // 3 for w in q]

    cand = (3 * col + 7) // 8
    place = jnp.minimum(40 * cand - TILE_COLS * col, TILE_COLS - 1)
    x_load.wait()
    cand_live = rank[0, place] < count[0, 0]
    lsrc[...] = jnp.where(
        cand_live, xv[:, pl.ds(pl.multiple_of(place * BLOCK, BLOCK), BLOCK)], 0.0
    )

    def p1_copy(d):
        to = lax.rem(y + d, N_Y)
        return remote(
            lsrc.at[pl.ds(to * PIECE, PIECE)], pa.at[y], p1_s.at[d - 1], p1_r.at[d - 1], at_y(to)
        )

    def p1_wait(d):
        frm = lax.rem(y + N_Y - d, N_Y)
        return remote(pa.at[frm], pa.at[frm], p1_s.at[d - 1], p1_r.at[d - 1], at_y(frm))

    for d in FAR_Y:
        p1_copy(d).start()
    pa[y] = lsrc[pl.ds(pl.multiple_of(y * PIECE, PIECE), PIECE), :]

    def p2_copy(t):
        return remote(pb.at[t], pc.at[x], p2_s.at[t], p2_r.at[x], at_x(t))

    def p2_wait(frm):
        return remote(pc.at[frm], pc.at[frm], p2_s.at[0], p2_r.at[frm], at_x(frm))

    def p3_copy():
        return remote(pd, pe, p3_s.at[0], p3_r.at[0], other_zh)

    def p4_slot(t):
        return ph.at[:, pl.ds(pl.multiple_of(t * BLOCK, BLOCK), BLOCK)]

    def p4_copy(d):
        return remote(
            p4_slot(x), p4_slot(x), p4_s.at[d - 1], p4_r.at[d - 1], at_x(lax.rem(x + d, N_X))
        )

    def p4_wait(d):
        frm = lax.rem(x + N_X - d, N_X)
        return remote(p4_slot(frm), p4_slot(frm), p4_s.at[d - 1], p4_r.at[d - 1], at_x(frm))

    def left_rows(yy):
        return left.at[pl.ds(pl.multiple_of(yy * PIECE, PIECE), PIECE), :]

    def p5_copy(d):
        return remote(
            ph, left_rows(y), p5_s.at[d - 1], p5_r.at[d - 1], at_y(lax.rem(y + d, N_Y))
        )

    def p5_wait(d):
        frm = lax.rem(y + N_Y - d, N_Y)
        return remote(left_rows(frm), left_rows(frm), p5_s.at[d - 1], p5_r.at[d - 1], at_y(frm))

    def phase_1_to_2():
        for d in range(1, N_Y):
            p1_wait(d).wait_recv()
        for t in range(ROUNDS):
            pb[t] = pa[(owner_col[t] // 2) % N_Y]
        for t in range(ROUNDS):
            @pl.when(x != t)
            def _(t=t):
                p2_copy(t).start()

            @pl.when(x == t)
            def _(t=t):
                pc[t] = pb[t]

    my_owner = jnp.where(x == 0, owner_col[0], jnp.where(x == 1, owner_col[1], owner_col[2]))

    def phase_2_to_3():
        @pl.when(x < ROUNDS)
        def _():
            for frm in range(N_X):
                @pl.when(x != frm)
                def _(frm=frm):
                    p2_wait(frm).wait_recv()
            pd[...] = pc[my_owner // (2 * N_Y)]
            p3_copy().start()

    def phase_3_to_4():
        @pl.when(x < ROUNDS)
        def _():
            p3_copy().wait_recv()
            mine = jnp.where(my_owner % 2 == zh, pd[...], pe[...])
            ph[:, pl.ds(pl.multiple_of(x * BLOCK, BLOCK), BLOCK)] = mine
            for d in range(1, N_X):
                p4_copy(d).start()

    def phase_4_to_5():
        for d in range(1, N_X):
            @pl.when(lax.rem(x + N_X - d, N_X) < ROUNDS)
            def _(d=d):
                p4_wait(d).wait_recv()
        left[pl.ds(pl.multiple_of(y * PIECE, PIECE), PIECE), :] = ph[...]
        for d in FAR_Y:
            p5_copy(d).start()

    def split(value):
        high = value.astype(jnp.bfloat16)
        return high, (value - high.astype(jnp.float32)).astype(jnp.bfloat16)

    def phase_5_end():
        for d in range(1, N_Y):
            p5_wait(d).wait_recv()
        left_high[...], left_low[...] = split(left[...])

    def up_copy(u, h):
        return remote(up.at[u, h], up.at[u, h], up_s.at[u, h], up_r.at[u, h], above)

    def down_copy(u, h):
        return remote(down.at[u, h], down.at[u, h], dn_s.at[u, h], dn_r.at[u, h], below)

    def sib_slot(j, half):
        rows = pl.ds(pl.multiple_of(half * HALF, HALF), HALF)
        return panels.at[pl.ds(j * ROUNDS, ROUNDS), rows, :]

    def sib_copy(j):
        return remote(sib_slot(j, core), sib_slot(j, core), sib_s.at[j], sib_r.at[j], sibling)

    def sib_wait(j):
        return remote(
            sib_slot(j, 1 - core), sib_slot(j, 1 - core), sib_s.at[j], sib_r.at[j], sibling
        )

    def window_of(t):
        return jnp.where(t == 0, q[0], jnp.where(t == 1, q[1], q[2]))

    def slot_of(u):
        late = jnp.maximum(u - 3 * TRIPLES, 0)
        third = (u * 43) >> 7
        half = late >> 1
        early = u < 3 * TRIPLES
        j = jnp.where(early, third, TRIPLES + half)
        t = jnp.where(early, u - 3 * third, late - 2 * half)
        return j, t

    def columns(j):
        return pl.ds(pl.multiple_of(j * BLOCK, BLOCK), BLOCK)

    def inject(buf, u, h, j, t):
        w = window_of(t)
        value = buf[u, h]
        for k in range(4):
            own = win[k, pl.ds(h * PART, PART), columns(j)]
            value = jnp.where(w == 4 * chip + k, own, value)
        buf[u, h] = value

    def wrap_copy(n, h):
        return remote(
            win.at[3, pl.ds(h * PART, PART), pl.ds((DOWN_LAST + n) * BLOCK, BLOCK)],
            relay.at[n, h], wr_s.at[n, h], rl_r.at[n, h], at_z(lax.rem(z + 4, N_Z)),
        )

    def wrap_wait(n, h):
        dst = relay.at[n, h]
        return remote(dst, dst, wr_s.at[n, h], rl_r.at[n, h], at_z(lax.rem(z + 8, N_Z)))

    def relay_copy(n, h):
        slot = 3 * (WRAP_FIRST + n) + 2
        return remote(
            relay.at[n, h], up.at[slot, h], rl_s.at[n, h], up_r.at[slot, h],
            at_z(lax.rem(z + 3, N_Z)),
        )

    far = jnp.maximum(chip, CHIPS - 1 - chip)
    acc[...] = jnp.zeros_like(acc)

    for w in range(2):
        win_loads[w].wait()
        win_arrival(0, w).wait_recv()

    def dot(a, b):
        return jnp.dot(a, b, preferred_element_type=jnp.float32)

    def multiply(j):
        sib_wait(j).wait_recv()
        right = panels[pl.ds(j * ROUNDS, ROUNDS)].reshape(ROUNDS * BLOCK, BLOCK)
        high, low = split(right)
        product = dot(left_high[...], high) + dot(left_high[...], low) + dot(left_low[...], high)
        cols = pl.ds(pl.multiple_of(j * BLOCK, BLOCK), BLOCK)
        live = rank[0, j] < count[0, 0]
        update = jnp.where(live, 1.5 * xv[:, cols] - 0.5 * product, 0.0)
        out[:, cols] = update
        acc[...] += jnp.sum((update * update).reshape(BLOCK // 8, 8, BLOCK), axis=0)

    def step(s, j):
        @pl.when(s == 9)
        def _():
            for w in range(2):
                win_loads[2 + w].wait()
                win_arrival(1, w).wait_recv()

        @pl.when((s == 10) & (chip == CHIPS - 1))
        def _():
            for n in range(WRAPS):
                for h in range(SUB):
                    wrap_copy(n, h).start()

        @pl.when((s >= RELAY_STEP) & (s < RELAY_STEP + WRAPS) & (chip == 3))
        def _():
            n = s - RELAY_STEP
            for h in range(SUB):
                wrap_wait(n, h).wait_recv()
                relay_copy(n, h).start()

        u = s - chip * LAG
        uj, ut = slot_of(jnp.clip(u, 0, SLOTS - 1))

        @pl.when((u >= 0) & (u < SLOTS) & (ut < 2))
        def _():
            for h in range(SUB):
                @pl.when(chip > 0)
                def _():
                    up_copy(u, h).wait_recv()

                inject(up, u, h, uj, ut)

                @pl.when(chip < CHIPS - 1)
                def _():
                    up_copy(u, h).start()

        @pl.when((u >= 0) & (u < SLOTS) & (ut == 2) & (uj >= WRAP_FIRST) & (chip < CHIPS - 1))
        def _():
            for h in range(SUB):
                up_copy(u, h).wait_recv()

                @pl.when(chip < CHIPS - 2)
                def _():
                    up_copy(u, h).start()

        d = s - (CHIPS - 1 - chip) * LAG
        dj, dt = slot_of(jnp.clip(d, 0, SLOTS - 1))

        @pl.when((d >= 0) & (d < SLOTS) & ((dt < 2) | (dj < DOWN_LAST)))
        def _():
            for h in range(SUB):
                @pl.when(chip < CHIPS - 1)
                def _():
                    down_copy(d, h).wait_recv()

                inject(down, d, h, dj, dt)

                @pl.when(chip > 0)
                def _():
                    down_copy(d, h).start()

        f = s - far * LAG

        fj, ft = slot_of(jnp.clip(f, 0, SLOTS - 1))

        def finish(j, t, value):
            unit = ROUNDS * j + t
            panels[unit, pl.ds(pl.multiple_of(core * HALF, HALF), HALF), :] = value

        @pl.when((f >= 0) & (f < SLOTS) & ((ft < 2) | (fj < DOWN_LAST)))
        def _():
            value = jnp.where(window_of(ft) // 4 < chip, up[f], down[f])
            finish(fj, ft, value.reshape(HALF, BLOCK))

            @pl.when(ft == jnp.where(fj < DOWN_LAST, 2, 1))
            def _():
                sib_copy(fj).start()

        wraps = (f >= 0) & (f < SLOTS) & (ft == 2) & (fj >= WRAP_FIRST)
        wrapped = fj + DOWN_LAST - WRAP_FIRST

        @pl.when(wraps & (chip < CHIPS - 1))
        def _():
            finish(wrapped, 2, up[f].reshape(HALF, BLOCK))

        @pl.when(wraps & (chip == CHIPS - 1))
        def _():
            finish(wrapped, 2, win[3, :, columns(wrapped)])

        for at, phase in zip(
            PHASES, (phase_1_to_2, phase_2_to_3, phase_3_to_4, phase_4_to_5, phase_5_end)
        ):
            pl.when(s == at)(phase)

        ready = (
            (j < TILE_COLS)
            & (s >= MM_FIRST + 2 * j)
            & (s >= jnp.minimum(3 * j + 2, 2 * j + TRIPLES + 1) + far * LAG + SIB_LAG)
        )

        @pl.when(ready)
        def _():
            multiply(j)

        return j + ready.astype(jnp.int32)

    lax.fori_loop(0, STEPS, step, jnp.int32(0))

    store = pltpu.make_async_copy(out, out_hbm, load_sem.at[1])
    store.start()

    sib_sum = remote(acc, qs.at[0], qs_s.at[0], qs_r.at[0], sibling)
    sib_sum.start()

    for copy in win_sends:
        copy.wait_send()
    for d in range(1, N_Y):
        p1_copy(d).wait_send()
        p5_copy(d).wait_send()
    for t in range(ROUNDS):
        @pl.when(x != t)
        def _(t=t):
            p2_copy(t).wait_send()

    @pl.when(x < ROUNDS)
    def _():
        p3_copy().wait_send()
        for d in range(1, N_X):
            p4_copy(d).wait_send()

    sib_sum.wait()
    qz[z] = acc[...] + qs[0]
    z_sums = [
        remote(qz.at[z], qz.at[z], qz_s.at[d - 1], qz_r.at[d - 1], peer)
        for d, peer in zip(FAR_Z, z_peers)
    ]
    for copy in z_sums:
        copy.start()

    def drain(u, carry):
        j, t = slot_of(u)

        @pl.when(
            (chip < CHIPS - 1) & (t < 2) | (chip < CHIPS - 2) & (t == 2) & (j >= WRAP_FIRST)
        )
        def _():
            for h in range(SUB):
                up_copy(u, h).wait_send()

        @pl.when((chip > 0) & ((t < 2) | (j < DOWN_LAST)))
        def _():
            for h in range(SUB):
                down_copy(u, h).wait_send()

        return carry

    lax.fori_loop(0, SLOTS, drain, 0)

    def drain_sib(u, carry):
        sib_copy(u).wait_send()
        return carry

    lax.fori_loop(0, TILE_COLS, drain_sib, 0)
    for n in range(WRAPS):
        @pl.when(chip == CHIPS - 1)
        def _(n=n):
            for h in range(SUB):
                wrap_copy(n, h).wait_send()

        @pl.when(chip == 3)
        def _(n=n):
            for h in range(SUB):
                relay_copy(n, h).wait_send()

    for d in range(1, N_Z):
        frm = lax.rem(z + N_Z - d, N_Z)
        remote(qz.at[frm], qz.at[frm], qz_s.at[d - 1], qz_r.at[d - 1], at_z(frm)).wait_recv()
    qy[y] = jnp.sum(qz[...], axis=0)
    y_sums = [
        remote(qy.at[y], qy.at[y], qy_s.at[d - 1], qy_r.at[d - 1], peer)
        for d, peer in zip(FAR_Y, y_peers)
    ]
    for copy in y_sums:
        copy.start()
    for d in range(1, N_Y):
        frm = lax.rem(y + N_Y - d, N_Y)
        remote(qy.at[frm], qy.at[frm], qy_s.at[d - 1], qy_r.at[d - 1], at_y(frm)).wait_recv()
    qx[x] = jnp.sum(qy[...], axis=0)
    x_sums = [
        remote(qx.at[x], qx.at[x], qx_s.at[d - 1], qx_r.at[d - 1], peer)
        for d, peer in zip(FAR_X, x_peers)
    ]
    for copy in x_sums:
        copy.start()
    for d in range(1, N_X):
        frm = lax.rem(x + N_X - d, N_X)
        remote(qx.at[frm], qx.at[frm], qx_s.at[d - 1], qx_r.at[d - 1], at_x(frm)).wait_recv()
    total[0, 0] = jnp.sum(jnp.sum(qx[...], axis=0))
    for copy in z_sums + y_sums + x_sums:
        copy.wait_send()
    store.wait()


def hand_over(updated, total, updated_out, total_out, held, sems):
    rows = BLOCK // 4
    parts = [pl.ds(n * rows, rows) for n in range(4)]
    loads = [
        pltpu.make_async_copy(updated.at[part], held.at[part], sems.at[0, n])
        for n, part in enumerate(parts)
    ]
    stores = [
        pltpu.make_async_copy(held.at[part], updated_out.at[part], sems.at[1, n])
        for n, part in enumerate(parts)
    ]
    for load in loads:
        load.start()
    total_out[0, 0] = total[0, 0]
    for load, store in zip(loads, stores):
        load.wait()
        store.start()
    for store in stores:
        store.wait()


def on_device(x_window, square_rows, block_rank, block_count, panel_order):
    width = TILE_COLS * BLOCK
    vmem = lambda *shape: pltpu.VMEM(shape, jnp.float32)
    dma = lambda *shape: pltpu.SemaphoreType.DMA(shape)
    updated, total = pl.pallas_call(
        kernel,
        out_shape=(
            jax.ShapeDtypeStruct((BLOCK, width), jnp.float32),
            jax.ShapeDtypeStruct((1, 1), jnp.float32),
        ),
        in_specs=[pl.BlockSpec(memory_space=pl.ANY)] * 5,
        out_specs=(
            pl.BlockSpec(memory_space=pl.ANY),
            pl.BlockSpec(memory_space=pltpu.SMEM),
        ),
        scratch_shapes=[
            pltpu.SMEM((ROUNDS,), jnp.int32),
            pltpu.SMEM((1, TILE_COLS), jnp.int32),
            pltpu.SMEM((1, 1), jnp.int32),
            vmem(BLOCK, width),
            vmem(4, HALF, width),
            vmem(SLOTS, SUB, PART, BLOCK),
            vmem(SLOTS, SUB, PART, BLOCK),
            vmem(WRAPS, SUB, PART, BLOCK),
            vmem(UNITS, BLOCK, BLOCK),
            vmem(BLOCK, width),
            vmem(BLOCK, BLOCK),
            vmem(N_Y, PIECE, BLOCK),
            vmem(ROUNDS, PIECE, BLOCK),
            vmem(N_X, PIECE, BLOCK),
            vmem(PIECE, BLOCK),
            vmem(PIECE, BLOCK),
            vmem(PIECE, ROUNDS * BLOCK),
            vmem(BLOCK, ROUNDS * BLOCK),
            pltpu.VMEM((BLOCK, ROUNDS * BLOCK), jnp.bfloat16),
            pltpu.VMEM((BLOCK, ROUNDS * BLOCK), jnp.bfloat16),
            vmem(8, BLOCK),
            vmem(1, 8, BLOCK),
            vmem(N_Z, 8, BLOCK),
            vmem(N_Y, 8, BLOCK),
            vmem(N_X, 8, BLOCK),
            dma(3), dma(2), dma(2, 2), dma(2, 2), dma(2, 2),
            dma(SLOTS, SUB), dma(SLOTS, SUB), dma(SLOTS, SUB), dma(SLOTS, SUB),
            dma(WRAPS, SUB), dma(WRAPS, SUB), dma(WRAPS, SUB), dma(TILE_COLS), dma(TILE_COLS),
            dma(N_Y - 1), dma(N_Y - 1), dma(ROUNDS), dma(N_X), dma(1), dma(1),
            dma(N_X - 1), dma(N_X - 1), dma(N_Y - 1), dma(N_Y - 1),
            dma(1), dma(1), dma(N_Z - 1), dma(N_Z - 1),
            dma(N_Y - 1), dma(N_Y - 1), dma(N_X - 1), dma(N_X - 1),
        ],
        compiler_params=pltpu.CompilerParams(
            collective_id=0, has_side_effects=True, vmem_limit_bytes=62 << 20
        ),
        name="sign_window",
    )(panel_order, block_rank, block_count, x_window, square_rows)
    updated, total = pl.pallas_call(
        hand_over,
        out_shape=(
            jax.ShapeDtypeStruct((BLOCK, width), jnp.float32),
            jax.ShapeDtypeStruct((1, 1), jnp.float32),
        ),
        in_specs=[pl.BlockSpec(memory_space=pl.ANY), pl.BlockSpec(memory_space=pltpu.SMEM)],
        out_specs=(
            pl.BlockSpec(memory_space=pl.ANY),
            pl.BlockSpec(memory_space=pltpu.SMEM),
        ),
        scratch_shapes=[vmem(BLOCK, width), dma(2, 4)],
        compiler_params=pltpu.CompilerParams(vmem_limit_bytes=62 << 20),
        name="hand_over",
    )(updated, total)
    return updated, total[0, 0]


def solution(mesh):
    return jax.shard_map(
        on_device,
        mesh=mesh,
        in_specs=(P("row", "col"), P("row", "col"), P("row", "col"), P("row", "col"), P()),
        out_specs=(P("row", "col"), P()),
        check_vma=False,
    )
```
